32 devices in a mesh: cell: 16 (over z, y, x), gpt: 2 (over core).
Axes of the slice: x: 2, y: 2, z: 4, core: 2. Of those that a mesh axis runs over, the one named last changes fastest.
Arguments:
- fields: bfloat16 [6, 16, 131072], P(None, None, 'cell'), may hold values from 0.00099 to 0.1002, as said below
- surface: bfloat16 [2, 131072], P(None, 'cell'), may hold values from 0.19921875 to 0.94921875
- sunlit: int32 [131072], P('cell'), may hold values from 0 to 1
- routing: int32 [1024], P('cell'), may hold values from -1 to 15, as said below
- stencil: int32 [7, 131072], P(None, 'cell'), may hold values from -128 to 128
- weights: float32 [7, 131072], P(None, 'cell'), may hold values from 0.1 to 1
- optics: float32 [3, 112], P(None, 'gpt'), may hold values from 0.05 to 20
- solar_flux: float32 [112], P('gpt'), may hold values from 0.5 to 2
Outputs:
- heating_rate: float32 [16, 131072], P('gpt', 'cell')
The draws below stay inside these ranges and needn't reach their ends.
Inputs may be any that keep to these rules, and one draw needn't show every extreme that they name: `routing`: each device is named by exactly 32 blocks in all, and by at most 4 of the 64 blocks of any one device. All fields are positive.
All inputs are finite; a program needn't handle non-finite values.
Results may differ from the reference program's by a relative error of at most 0.0003.
Values may be sent and summed in bfloat16 or wider, within the bound.
A program may use at most 64 MiB of HBM per device.

```python
import math
import jax
import jax.numpy as jnp
from jax import lax

G = 112
L = 16
BLK = 128
NB = 64
STEN = 7
HW = 128
NCOL = 131072
N_CELL = 16


def route_plan(key):
    half_cells = N_CELL // 2
    layers = NB // N_CELL
    key_shift, key_moved, key_flip, key_shuffle = jax.random.split(jax.random.fold_in(key, 11), 4)
    shift_value = jax.random.randint(key_shift, (), 0, N_CELL)
    moved = jax.random.randint(key_moved, (layers, half_cells), 0, half_cells + 1).at[:, 0].set(half_cells)
    flipped = jax.random.randint(key_flip, (half_cells,), 0, 2)
    source_ids = jnp.arange(N_CELL, dtype=jnp.int32)[:, None]
    target_ids = jnp.arange(N_CELL, dtype=jnp.int32)[None, :]
    pair_index = source_ids % half_cells
    taker = (source_ids < half_cells) != (flipped[pair_index] == 1)
    partner = (source_ids + half_cells) % N_CELL
    offset_own = (target_ids - source_ids - shift_value) % N_CELL
    offset_partner = (target_ids - partner - shift_value) % N_CELL
    base_plan = offset_own < half_cells
    move_count = moved[:, pair_index[:, 0]][:, :, None]
    losing = jnp.logical_not(taker)[None] & (offset_own[None] < move_count)
    gaining = taker[None] & (offset_partner[None] < move_count)
    assignment = base_plan[None] & jnp.logical_not(losing) | gaining
    counts = jnp.sum(assignment.astype(jnp.int32), axis=0)
    running = jnp.cumsum(counts, axis=1)
    sent_count = running[:, -1]
    position = jnp.arange(NB, dtype=jnp.int32)
    target_of = jnp.sum((running[:, None, :] <= position[None, :, None]).astype(jnp.int32), axis=2)
    assigned = jnp.where(position[None, :] < sent_count[:, None], target_of, -1).astype(jnp.int32)
    shuffles = jax.vmap(lambda each_key: jax.random.permutation(each_key, NB))(jax.random.split(key_shuffle, N_CELL))
    destination = jnp.take_along_axis(assigned, shuffles.astype(jnp.int32), axis=1)
    return destination.reshape(-1).astype(jnp.int32)


def draw_routing(key, part):
    return route_plan(key)


def draw_sunlit(key, part):
    light_draw = jax.random.randint(jax.random.fold_in(key, 13), (NCOL,), 0, 20) < 17
    return light_draw.astype(jnp.int32)


def draw_stencil(key, part):
    offsets = jax.random.randint(jax.random.fold_in(key, 23), (STEN, NCOL), -HW, HW + 1)
    offsets = offsets.at[0, 0].set(-HW)
    offsets = offsets.at[1, 1].set(HW)
    return offsets.astype(jnp.int32)


def draw_fields(key, part):
    lower_ends = jnp.array([0.02, 0.005, 0.002, 0.001, 0.001, 0.001], jnp.float32)[:, None, None]
    upper_ends = jnp.array([0.06, 0.1, 0.02, 0.1, 0.05, 0.01], jnp.float32)[:, None, None]
    uniform_draw = jax.random.uniform(jax.random.fold_in(key, 31), (6, L, NCOL), jnp.float32)
    values = lower_ends * jnp.exp(uniform_draw * jnp.log(upper_ends / lower_ends))
    return values.astype(jnp.bfloat16)


def block_scale(rng, dims, cuts, smallest, largest):
    factor_of = 1.0
    for dim, parts in cuts:
        heights = jax.random.uniform(jax.random.fold_in(jax.random.fold_in(rng, 6), dim), (parts,), jnp.float32, smallest / len(cuts), largest / len(cuts))
        factor_of = factor_of * jnp.repeat(jnp.exp(heights), dims[dim] // parts).reshape((-1,) + (1,) * (len(dims) - 1 - dim))
    return factor_of


def setup_inputs(seed: int = 0) -> dict:
    keys = jax.random.split(jax.random.key(seed), 9)
    fields = draw_fields(jax.random.fold_in(keys[8], 71), 0)
    surface = jnp.clip(0.19921875 + 0.75 * jax.random.uniform(keys[1], (2, NCOL), jnp.float32) ** block_scale(keys[1], (2, NCOL), ((1, 16),), -0.2, 0.2), 0.19921875, 0.94921875).astype(jnp.bfloat16)
    sunlit = draw_sunlit(jax.random.fold_in(keys[8], 71), 0)
    routing = draw_routing(jax.random.fold_in(keys[8], 71), 0)
    stencil = draw_stencil(jax.random.fold_in(keys[8], 71), 0)
    weights = jnp.clip(0.1 + 0.9 * jax.random.uniform(keys[5], (STEN, NCOL), jnp.float32) ** block_scale(keys[5], (STEN, NCOL), ((1, 16),), -0.2, 0.2), 0.1, 1.0)
    optics = jnp.clip(jnp.exp(math.log(20.0) - 5.9914645 * jax.random.uniform(keys[6], (3, G), jnp.float32) ** block_scale(keys[6], (3, G), ((1, 2),), -0.2, 0.2)), 0.05, 20.0)
    solar_flux = jnp.clip(jnp.exp(math.log(2.0) - 1.3862944 * jax.random.uniform(keys[7], (G,), jnp.float32) ** block_scale(keys[7], (G,), ((0, 2),), -0.2, 0.2)), 0.5, 2.0)
    return dict(fields=fields, surface=surface, sunlit=sunlit, routing=routing, stencil=stencil, weights=weights, optics=optics, solar_flux=solar_flux)


def column_heat(fields, geometry, optics, solar_flux, factor):
    levels = fields.shape[1]
    cosine = geometry[0].astype(jnp.float32)[None, :]
    albedo = geometry[1].astype(jnp.float32)[None, :]
    lit_part = geometry[2].astype(jnp.float32)[None, :]
    k_vapor = optics[0][:, None]
    k_ozone = optics[1][:, None]
    k_rayleigh = optics[2][:, None]
    incoming = solar_flux[:, None] * lit_part * cosine
    optical_depth = jnp.zeros_like(incoming)
    scattering = []
    absorbed = []
    direct = []
    for layer_index in range(levels):
        column = fields[:, layer_index].astype(jnp.float32)
        clouds = column[3] + column[4]
        scatter_now = k_rayleigh * column[0] + 0.9 * clouds + 0.8 * column[5]
        absorb_now = k_vapor * column[1] + k_ozone * column[2] + 0.1 * clouds + 0.2 * column[5]
        optical_depth = optical_depth + scatter_now + absorb_now
        scattering.append(scatter_now)
        absorbed.append(absorb_now)
        direct.append(incoming * jnp.exp(-optical_depth / cosine))
    coupling = [0.5 * (scattering[i] + scattering[i + 1]) + 0.1 for i in range(levels - 1)]
    ratios = []
    partial_sol = []
    for layer_index in range(levels):
        above = coupling[layer_index - 1] if layer_index > 0 else 0.5
        below = coupling[layer_index] if layer_index < levels - 1 else 0.5
        diagonal = absorbed[layer_index] + above + below
        source = scattering[layer_index] * direct[layer_index]
        if layer_index == levels - 1:
            source = source + albedo * direct[layer_index]
        if layer_index > 0:
            pivots = diagonal - above * ratios[layer_index - 1]
            solved = (source + above * partial_sol[layer_index - 1]) / pivots
        else:
            pivots = diagonal
            solved = source / pivots
        ratios.append(below / pivots)
        partial_sol.append(solved)
    diffuse = partial_sol[levels - 1]
    heat_rows = [None] * levels
    for layer_index in reversed(range(levels)):
        if layer_index < levels - 1:
            diffuse = partial_sol[layer_index] + ratios[layer_index] * diffuse
        heat_rows[layer_index] = jnp.sum(absorbed[layer_index] * (diffuse + direct[layer_index]), axis=0) * factor
    return jnp.stack(heat_rows)


def reference(fields, surface, sunlit, routing, stencil, weights, optics, solar_flux):
    column_total = fields.shape[2]
    block_total = column_total // BLK
    routed = jnp.repeat((routing >= 0).astype(jnp.float32), BLK)
    geometry = jnp.stack([surface[0].astype(jnp.float32), surface[1].astype(jnp.float32), sunlit.astype(jnp.float32) * routed])
    field_blocks = jnp.moveaxis(fields.reshape(6, L, block_total, BLK), 2, 0)
    geometry_blocks = jnp.moveaxis(geometry.reshape(3, block_total, BLK), 1, 0)
    factor = 1.0 / G

    def one_block(pieces):
        return column_heat(pieces[0], pieces[1], optics, solar_flux, factor)

    heating = lax.map(one_block, (field_blocks, geometry_blocks))
    heating = jnp.moveaxis(heating, 0, 1).reshape(L, column_total)
    normalized = weights / jnp.sum(weights, axis=0, keepdims=True)
    neighbour = (jnp.arange(column_total, dtype=jnp.int32)[None, :] + stencil) % column_total
    result = jnp.zeros((L, column_total), jnp.float32)
    for stencil_point in range(STEN):
        result = result + normalized[stencil_point][None, :] * heating[:, neighbour[stencil_point]]
    return result
```

```python
import functools
import math

import jax
import jax.numpy as jnp
from jax import lax
from jax.experimental import pallas as pl
from jax.experimental.pallas import tpu as pltpu
from jax.sharding import PartitionSpec as P

G = 112
BLK = 128
HW = 128
ROWS = 8
WIDE = ROWS * BLK
LOG2E = math.log2(math.e)


def solve_kernel(
    levels,
    per_step,
    group_of,
    core_ref,
    routing_ref,
    optics_ref,
    flux_ref,
    fields_ref,
    surface_ref,
    sunlit_ref,
    keep_ref,
    send_ref,
    natural,
    packed,
    rows,
    total,
    turned,
):
    bands = flux_ref.shape[0]
    group = group_of(pl.program_id(0))
    core = core_ref[0]

    for b in range(ROWS):
        cols = pl.ds(b * BLK, BLK)
        here = pl.ds(b * levels, levels)
        cosine = surface_ref[0:1, cols].astype(jnp.float32)
        albedo = surface_ref[1:2, cols].astype(jnp.float32)
        scale = -LOG2E / cosine
        f = [fields_ref[k, :, cols].astype(jnp.float32) for k in range(6)]
        clouds = f[3] + f[4]
        natural[0, here, :] = scale * f[0]
        natural[1, here, :] = scale * f[1]
        natural[2, here, :] = scale * f[2]
        natural[3, here, :] = scale * (0.9 * clouds + 0.8 * f[5])
        natural[4, here, :] = scale * (0.1 * clouds + 0.2 * f[5])
        rows[0, b : b + 1, :] = scale
        rows[1, b : b + 1, :] = albedo * scale

    for level in range(levels):
        for k in range(5):
            packed[k, level] = natural[k, pl.ds(level, ROWS, stride=levels), :]
    scale = rows[0]
    for level in range(levels - 1):
        packed[5, level] = 0.5 * (packed[0, level] + packed[0, level + 1])
        packed[6, level] = 0.5 * (packed[3, level] + packed[3, level + 1]) + 0.1 * scale
    for level in range(levels):
        total[level] = jnp.zeros((ROWS, BLK), jnp.float32)

    def some_bands(step, carry):
        first = step * per_step
        lanes = range(per_step)
        kv = [optics_ref[0, first + i] for i in lanes]
        ko = [optics_ref[1, first + i] for i in lanes]
        kr = [optics_ref[2, first + i] for i in lanes]
        t = [LOG2E * jnp.log(jnp.full((ROWS, BLK), flux_ref[first + i], jnp.float32)) for i in lanes]
        half = 0.5 * rows[0]
        ratio = [None] * per_step
        rest = [None] * per_step
        filled = [None] * per_step
        kept = [[] for _ in lanes]
        for level in range(levels):
            last = level == levels - 1
            f0, f1, f2, cs, ca = [packed[k, level] for k in range(5)]
            if not last:
                f5, f6 = packed[5, level], packed[6, level]
            for i in lanes:
                s = kr[i] * f0 + cs
                a = kv[i] * f1 + (ko[i] * f2 + ca)
                t[i] = t[i] + (s + a)
                d = jnp.exp2(t[i])
                c = half if last else kr[i] * f5 + f6
                q = a + (half if level == 0 else ratio[i] * rest[i])
                inverse = pl.reciprocal(q + c, approx=True)
                z = ((s + rows[1]) if last else s) * d
                if level > 0:
                    z = z + ratio[i] * filled[i]
                rest[i], filled[i] = q, z
                ratio[i] = c * inverse
                kept[i].append((a, d, ratio[i], z * inverse))
        x = [None] * per_step
        for level in reversed(range(levels)):
            heat = total[level]
            for i in lanes:
                a, d, r, y = kept[i][level]
                x[i] = y if level == levels - 1 else y + r * x[i]
                heat = heat + a * (x[i] + d)
            total[level] = heat
        return carry

    lax.fori_loop(0, bands // per_step, some_bands, 0)

    for level in range(levels):
        turned[pl.ds(level, ROWS, stride=levels), :] = total[level]
    half_levels = levels // 2
    for b in range(ROWS):
        cols = pl.ds(b * BLK, BLK)
        cosine = surface_ref[0:1, cols].astype(jnp.float32)
        routed = (routing_ref[group * ROWS + b] >= 0).astype(jnp.float32)
        lit = sunlit_ref[b : b + 1, :].astype(jnp.float32) * routed
        weight = lit * (cosine * cosine) * (-1.0 / (LOG2E * G))
        mine = pl.multiple_of(b * levels + core * half_levels, half_levels)
        other = pl.multiple_of(b * levels + (1 - core) * half_levels, half_levels)
        keep_ref[:, cols] = turned[pl.ds(mine, half_levels), :] * weight
        send_ref[:, cols] = turned[pl.ds(other, half_levels), :] * weight


def solve_groups(core, routing, optics, flux, fields, surface, sunlit, group_of, count, per_step):
    levels = fields.shape[1]
    bands = flux.shape[0]
    half_levels = levels // 2
    smem = pl.BlockSpec(memory_space=pltpu.SMEM)
    out = pl.BlockSpec((half_levels, WIDE), lambda i: (0, i))
    shape = jax.ShapeDtypeStruct((half_levels, count * WIDE), jnp.float32)
    elements = count * WIDE * levels * bands
    return pl.pallas_call(
        functools.partial(solve_kernel, levels, per_step, group_of),
        grid=(count,),
        in_specs=[
            smem,
            smem,
            smem,
            smem,
            pl.BlockSpec((6, levels, WIDE), lambda i: (0, 0, group_of(i))),
            pl.BlockSpec((2, WIDE), lambda i: (0, group_of(i))),
            pl.BlockSpec((ROWS, BLK), lambda i: (group_of(i), 0)),
        ],
        out_specs=[out, out],
        out_shape=[shape, shape],
        scratch_shapes=[
            pltpu.VMEM((5, ROWS * levels, BLK), jnp.float32),
            pltpu.VMEM((7, levels, ROWS, BLK), jnp.float32),
            pltpu.VMEM((2, ROWS, BLK), jnp.float32),
            pltpu.VMEM((levels, ROWS, BLK), jnp.float32),
            pltpu.VMEM((ROWS * levels, BLK), jnp.float32),
        ],
        cost_estimate=pl.CostEstimate(
            flops=elements * 24, bytes_accessed=count * WIDE * levels * 20, transcendentals=elements * 2
        ),
    )(core, routing, optics, flux, fields, surface, sunlit)


def interpolate_kernel(
    edge_ref, edge_in_ref, mid_ref, mid_in_ref, low_ref, high_ref, stencil_ref, weights_ref, out_ref, wide
):
    columns = out_ref.shape[1]
    points = stencil_ref.shape[0]
    blocks = columns // BLK
    wide[:, 0:HW] = low_ref[...]
    wide[:, HW + columns : 2 * HW + columns] = high_ref[...]
    wide[:, HW : HW + WIDE] = edge_ref[:, 0:WIDE] + edge_in_ref[:, 0:WIDE]
    wide[:, HW + columns - WIDE : HW + columns] = edge_ref[:, WIDE:] + edge_in_ref[:, WIDE:]
    wide[:, HW + WIDE : HW + columns - WIDE] = mid_ref[...] + mid_in_ref[...]
    lane = lax.broadcasted_iota(jnp.int32, (points, BLK), 1) + HW

    def one_block(block, carry):
        start = pl.multiple_of(block * BLK, BLK)
        weights = weights_ref[:, pl.ds(start, BLK)]
        shares = weights / jnp.sum(weights, axis=0, keepdims=True)
        place = stencil_ref[:, pl.ds(start, BLK)] + lane
        which = place >> 7
        inner = place & (BLK - 1)
        sources = [wide[:, pl.ds(pl.multiple_of(start + k * BLK, BLK), BLK)] for k in range(3)]
        result = jnp.zeros(sources[0].shape, jnp.float32)
        for j in range(points):
            index = jnp.broadcast_to(inner[j : j + 1, :], result.shape)
            part = jnp.broadcast_to(which[j : j + 1, :], result.shape)
            got = [jnp.take_along_axis(s, index, axis=1, mode="promise_in_bounds") for s in sources]
            value = jnp.where(part == 0, got[0], jnp.where(part == 1, got[1], got[2]))
            result = result + shares[j : j + 1, :] * value
        out_ref[:, pl.ds(start, BLK)] = result
        return carry

    lax.fori_loop(0, blocks, one_block, 0, unroll=4)


def interpolate(edge, edge_in, mid, mid_in, low, high, stencil, weights):
    half_levels = low.shape[0]
    columns = stencil.shape[1]
    return pl.pallas_call(
        interpolate_kernel,
        in_specs=[pl.BlockSpec(memory_space=pltpu.VMEM)] * 8,
        out_specs=pl.BlockSpec(memory_space=pltpu.VMEM),
        out_shape=jax.ShapeDtypeStruct((half_levels, columns), jnp.float32),
        scratch_shapes=[pltpu.VMEM((half_levels, columns + 2 * HW), jnp.float32)],
        compiler_params=pltpu.CompilerParams(vmem_limit_bytes=16 * 1024 * 1024),
    )(edge, edge_in, mid, mid_in, low, high, stencil, weights)


def local(fields, surface, sunlit, routing, stencil, weights, optics, solar_flux):
    columns = fields.shape[2]
    groups = columns // WIDE
    count = lax.axis_size("cell")
    core = lax.axis_index("gpt").reshape(1)
    lit = sunlit.reshape(columns // BLK, BLK)
    solve = functools.partial(solve_groups, core, routing, optics, solar_flux, fields, surface, lit)
    swap = [(0, 1), (1, 0)]
    up = [(i, (i + 1) % count) for i in range(count)]
    down = [(b, a) for a, b in up]
    edge, edge_out = solve(lambda i: i * (groups - 1), 2, 2)
    edge_in = lax.ppermute(edge_out, "gpt", swap)
    mid, mid_out = solve(lambda i: i + 1, groups - 2, 2)
    low = lax.ppermute(edge[:, -HW:] + edge_in[:, -HW:], "cell", up)
    high = lax.ppermute(edge[:, :HW] + edge_in[:, :HW], "cell", down)
    mid_in = lax.ppermute(mid_out, "gpt", swap)
    return interpolate(edge, edge_in, mid, mid_in, low, high, stencil, weights)


def solution(mesh):
    placed = (
        P(None, None, "cell"),
        P(None, "cell"),
        P("cell"),
        P("cell"),
        P(None, "cell"),
        P(None, "cell"),
        P(None, "gpt"),
        P("gpt"),
    )
    return jax.shard_map(
        local, mesh=mesh, in_specs=placed, out_specs=P("gpt", "cell"), check_vma=False
    )
```

```python
import functools
import math

import jax
import jax.numpy as jnp
from jax import lax
from jax.experimental import pallas as pl
from jax.experimental.pallas import tpu as pltpu
from jax.sharding import PartitionSpec as P

G = 112
BLK = 128
HW = 128
ROWS = 8
WIDE = ROWS * BLK
LOG2E = math.log2(math.e)


def solve_kernel(
    levels,
    per_step,
    group_of,
    core_ref,
    routing_ref,
    optics_ref,
    flux_ref,
    fields_ref,
    surface_ref,
    sunlit_ref,
    keep_ref,
    send_ref,
    natural,
    packed,
    rows,
    total,
    turned,
    slot_a,
    slot_b,
):
    bands = flux_ref.shape[0]
    group = group_of(pl.program_id(0))
    core = core_ref[0]

    for b in range(ROWS):
        cols = pl.ds(b * BLK, BLK)
        here = pl.ds(b * levels, levels)
        cosine = surface_ref[0:1, cols].astype(jnp.float32)
        albedo = surface_ref[1:2, cols].astype(jnp.float32)
        scale = -LOG2E / cosine
        f = [fields_ref[k, :, cols].astype(jnp.float32) for k in range(6)]
        clouds = f[3] + f[4]
        natural[0, here, :] = scale * f[0]
        natural[1, here, :] = scale * f[1]
        natural[2, here, :] = scale * f[2]
        natural[3, here, :] = scale * (0.9 * clouds + 0.8 * f[5])
        natural[4, here, :] = scale * (0.1 * clouds + 0.2 * f[5])
        rows[0, b : b + 1, :] = scale
        rows[1, b : b + 1, :] = albedo * scale

    for level in range(levels):
        for k in range(5):
            packed[k, level] = natural[k, pl.ds(level, ROWS, stride=levels), :]
    scale = rows[0]
    for level in range(levels - 1):
        packed[5, level] = 0.5 * (packed[0, level] + packed[0, level + 1])
        packed[6, level] = 0.5 * (packed[3, level] + packed[3, level + 1]) + 0.1 * scale
    for level in range(levels):
        total[level] = jnp.zeros((ROWS, BLK), jnp.float32)

    def ahead(step, slot):
        first = step * per_step
        lanes = range(per_step)
        kv = [optics_ref[0, first + i] for i in lanes]
        ko = [optics_ref[1, first + i] for i in lanes]
        kr = [optics_ref[2, first + i] for i in lanes]
        t = [LOG2E * jnp.log(jnp.full((ROWS, BLK), flux_ref[first + i], jnp.float32)) for i in lanes]
        half = 0.5 * rows[0]
        ratio = [None] * per_step
        rest = [None] * per_step
        filled = [None] * per_step
        for level in range(levels):
            last = level == levels - 1
            f0, f1, f2, cs, ca = [packed[k, level] for k in range(5)]
            if not last:
                f5, f6 = packed[5, level], packed[6, level]
            for i in lanes:
                s = kr[i] * f0 + cs
                a = kv[i] * f1 + (ko[i] * f2 + ca)
                t[i] = t[i] + (s + a)
                d = jnp.exp2(t[i])
                c = half if last else kr[i] * f5 + f6
                q = a + (half if level == 0 else ratio[i] * rest[i])
                inverse = pl.reciprocal(q + c, approx=True)
                z = ((s + rows[1]) if last else s) * d
                if level > 0:
                    z = z + ratio[i] * filled[i]
                rest[i], filled[i] = q, z
                ratio[i] = c * inverse
                slot[0, level, i] = a
                slot[1, level, i] = d
                slot[2, level, i] = z * inverse
                if not last:
                    slot[3, level, i] = ratio[i]
            yield

    def back(slot):
        x = [None] * per_step
        for level in reversed(range(levels)):
            heat = total[level]
            for i in range(per_step):
                y = slot[2, level, i]
                x[i] = y if level == levels - 1 else y + slot[3, level, i] * x[i]
                heat = heat + slot[0, level, i] * (x[i] + slot[1, level, i])
            total[level] = heat
            yield

    def run(*parts):
        for _ in zip(*parts):
            pass

    steps = bands // per_step
    run(ahead(0, slot_a))

    def two_steps(k, carry):
        run(ahead(2 * k + 1, slot_b), back(slot_a))
        run(ahead(2 * k + 2, slot_a), back(slot_b))
        return carry

    lax.fori_loop(0, (steps - 1) // 2, two_steps, 0)
    if steps % 2:
        run(back(slot_a))
    else:
        run(ahead(steps - 1, slot_b), back(slot_a))
        run(back(slot_b))

    for level in range(levels):
        turned[pl.ds(level, ROWS, stride=levels), :] = total[level]
    half_levels = levels // 2
    for b in range(ROWS):
        cols = pl.ds(b * BLK, BLK)
        cosine = surface_ref[0:1, cols].astype(jnp.float32)
        routed = (routing_ref[group * ROWS + b] >= 0).astype(jnp.float32)
        lit = sunlit_ref[b : b + 1, :].astype(jnp.float32) * routed
        weight = lit * (cosine * cosine) * (-1.0 / (LOG2E * G))
        mine = pl.multiple_of(b * levels + core * half_levels, half_levels)
        other = pl.multiple_of(b * levels + (1 - core) * half_levels, half_levels)
        keep_ref[:, cols] = turned[pl.ds(mine, half_levels), :] * weight
        send_ref[:, cols] = turned[pl.ds(other, half_levels), :] * weight


def solve_groups(core, routing, optics, flux, fields, surface, sunlit, group_of, count, per_step):
    levels = fields.shape[1]
    bands = flux.shape[0]
    half_levels = levels // 2
    smem = pl.BlockSpec(memory_space=pltpu.SMEM)
    out = pl.BlockSpec((half_levels, WIDE), lambda i: (0, i))
    shape = jax.ShapeDtypeStruct((half_levels, count * WIDE), jnp.float32)
    elements = count * WIDE * levels * bands
    return pl.pallas_call(
        functools.partial(solve_kernel, levels, per_step, group_of),
        grid=(count,),
        in_specs=[
            smem,
            smem,
            smem,
            smem,
            pl.BlockSpec((6, levels, WIDE), lambda i: (0, 0, group_of(i))),
            pl.BlockSpec((2, WIDE), lambda i: (0, group_of(i))),
            pl.BlockSpec((ROWS, BLK), lambda i: (group_of(i), 0)),
        ],
        out_specs=[out, out],
        out_shape=[shape, shape],
        scratch_shapes=[
            pltpu.VMEM((5, ROWS * levels, BLK), jnp.float32),
            pltpu.VMEM((7, levels, ROWS, BLK), jnp.float32),
            pltpu.VMEM((2, ROWS, BLK), jnp.float32),
            pltpu.VMEM((levels, ROWS, BLK), jnp.float32),
            pltpu.VMEM((ROWS * levels, BLK), jnp.float32),
            pltpu.VMEM((4, levels, per_step, ROWS, BLK), jnp.float32),
            pltpu.VMEM((4, levels, per_step, ROWS, BLK), jnp.float32),
        ],
        cost_estimate=pl.CostEstimate(
            flops=elements * 24, bytes_accessed=count * WIDE * levels * 20, transcendentals=elements * 2
        ),
    )(core, routing, optics, flux, fields, surface, sunlit)


def exchange_kernel(keep_ref, send_ref, near_ref, halo_ref, send_sem, recv_sem):
    count = lax.axis_size("cell")
    cell = lax.axis_index("cell")
    core = lax.axis_index("gpt")
    columns = keep_ref.shape[1]
    after, before = lax.rem(cell + 1, count), lax.rem(cell + count - 1, count)
    partners = [(cell, 1 - core), (after, core), (after, 1 - core), (before, core), (before, 1 - core)]
    barrier = pltpu.get_barrier_semaphore()
    for partner in partners:
        pl.semaphore_signal(barrier, inc=1, device_id=partner, device_id_type=pl.DeviceIdType.MESH)
    pl.semaphore_wait(barrier, len(partners))
    tail = pl.ds(columns - HW, HW)
    head = pl.ds(0, HW)
    copies = [
        (keep_ref.at[:, tail], halo_ref.at[0]),
        (send_ref.at[:, tail], halo_ref.at[1]),
        (keep_ref.at[:, head], halo_ref.at[2]),
        (send_ref.at[:, head], halo_ref.at[3]),
        (send_ref, near_ref),
    ]
    started = []
    for k, (source, target) in enumerate(copies):
        copy = pltpu.make_async_remote_copy(
            src_ref=source,
            dst_ref=target,
            send_sem=send_sem.at[k],
            recv_sem=recv_sem.at[k],
            device_id=(partners[1:] + partners[:1])[k],
            device_id_type=pl.DeviceIdType.MESH,
        )
        copy.start()
        started.append(copy)
    for copy in started:
        copy.wait()


def exchange(keep, send):
    half_levels = keep.shape[0]
    vmem = pl.BlockSpec(memory_space=pltpu.VMEM)
    return pl.pallas_call(
        exchange_kernel,
        in_specs=[vmem] * 2,
        out_specs=[vmem] * 2,
        out_shape=[
            jax.ShapeDtypeStruct(send.shape, jnp.float32),
            jax.ShapeDtypeStruct((4, half_levels, HW), jnp.float32),
        ],
        scratch_shapes=[pltpu.SemaphoreType.DMA((5,)), pltpu.SemaphoreType.DMA((5,))],
        compiler_params=pltpu.CompilerParams(collective_id=0, has_side_effects=True),
    )(keep, send)


def interpolate_kernel(keep_ref, near_ref, halo_ref, stencil_ref, weights_ref, out_ref, wide):
    columns = out_ref.shape[1]
    points = stencil_ref.shape[0]
    blocks = columns // BLK
    wide[:, 0:HW] = halo_ref[0] + halo_ref[1]
    wide[:, HW + columns : 2 * HW + columns] = halo_ref[2] + halo_ref[3]
    wide[:, HW : HW + columns] = keep_ref[...] + near_ref[...]
    lane = lax.broadcasted_iota(jnp.int32, (points, BLK), 1) + HW

    def one_block(block, carry):
        start = pl.multiple_of(block * BLK, BLK)
        weights = weights_ref[:, pl.ds(start, BLK)]
        shares = weights / jnp.sum(weights, axis=0, keepdims=True)
        place = stencil_ref[:, pl.ds(start, BLK)] + lane
        which = place >> 7
        inner = place & (BLK - 1)
        sources = [wide[:, pl.ds(pl.multiple_of(start + k * BLK, BLK), BLK)] for k in range(3)]
        result = jnp.zeros(sources[0].shape, jnp.float32)
        for j in range(points):
            index = jnp.broadcast_to(inner[j : j + 1, :], result.shape)
            part = jnp.broadcast_to(which[j : j + 1, :], result.shape)
            got = [jnp.take_along_axis(s, index, axis=1, mode="promise_in_bounds") for s in sources]
            value = jnp.where(part == 0, got[0], jnp.where(part == 1, got[1], got[2]))
            result = result + shares[j : j + 1, :] * value
        out_ref[:, pl.ds(start, BLK)] = result
        return carry

    lax.fori_loop(0, blocks, one_block, 0, unroll=4)


def interpolate(*operands):
    half_levels = operands[0].shape[0]
    columns = operands[-1].shape[1]
    return pl.pallas_call(
        interpolate_kernel,
        in_specs=[pl.BlockSpec(memory_space=pltpu.VMEM)] * len(operands),
        out_specs=pl.BlockSpec(memory_space=pltpu.VMEM),
        out_shape=jax.ShapeDtypeStruct((half_levels, columns), jnp.float32),
        scratch_shapes=[pltpu.VMEM((half_levels, columns + 2 * HW), jnp.float32)],
        compiler_params=pltpu.CompilerParams(vmem_limit_bytes=16 * 1024 * 1024),
    )(*operands)


def local(fields, surface, sunlit, routing, stencil, weights, optics, solar_flux):
    columns = fields.shape[2]
    groups = columns // WIDE
    core = lax.axis_index("gpt").reshape(1)
    lit = sunlit.reshape(columns // BLK, BLK)
    solve = functools.partial(solve_groups, core, routing, optics, solar_flux, fields, surface, lit)
    keep, send = solve(lambda i: i, groups, 4)
    near, halo = exchange(keep, send)
    return interpolate(keep, near, halo, stencil, weights)


def solution(mesh):
    placed = (
        P(None, None, "cell"),
        P(None, "cell"),
        P("cell"),
        P("cell"),
        P(None, "cell"),
        P(None, "cell"),
        P(None, "gpt"),
        P("gpt"),
    )
    return jax.shard_map(
        local, mesh=mesh, in_specs=placed, out_specs=P("gpt", "cell"), check_vma=False
    )
```

```python
import functools
import math

import jax
import jax.numpy as jnp
from jax import lax
from jax.experimental import pallas as pl
from jax.experimental.pallas import tpu as pltpu
from jax.sharding import PartitionSpec as P

G = 112
BLK = 128
HW = 128
ROWS = 8
WIDE = ROWS * BLK
LOG2E = math.log2(math.e)


def solve_kernel(
    levels,
    per_step,
    group_of,
    core_ref,
    routing_ref,
    optics_ref,
    flux_ref,
    fields_ref,
    surface_ref,
    sunlit_ref,
    keep_ref,
    send_ref,
    natural,
    packed,
    rows,
    total,
    turned,
    slot_a,
    slot_b,
):
    bands = flux_ref.shape[0]
    group = group_of(pl.program_id(0))
    core = core_ref[0]

    for b in range(ROWS):
        cols = pl.ds(b * BLK, BLK)
        here = pl.ds(b * levels, levels)
        cosine = surface_ref[0:1, cols].astype(jnp.float32)
        albedo = surface_ref[1:2, cols].astype(jnp.float32)
        scale = -LOG2E / cosine
        f = [fields_ref[k, :, cols].astype(jnp.float32) for k in range(6)]
        clouds = f[3] + f[4]
        natural[0, here, :] = scale * f[0]
        natural[1, here, :] = scale * f[1]
        natural[2, here, :] = scale * f[2]
        natural[3, here, :] = scale * (0.9 * clouds + 0.8 * f[5])
        natural[4, here, :] = scale * (0.1 * clouds + 0.2 * f[5])
        rows[0, b : b + 1, :] = scale
        rows[1, b : b + 1, :] = albedo * scale

    for level in range(levels):
        for k in range(5):
            packed[k, level] = natural[k, pl.ds(level, ROWS, stride=levels), :]
    scale = rows[0]
    for level in range(levels - 1):
        packed[5, level] = 0.5 * (packed[0, level] + packed[0, level + 1])
        packed[6, level] = 0.5 * (packed[3, level] + packed[3, level + 1]) + 0.1 * scale
    for level in range(levels):
        total[level] = jnp.zeros((ROWS, BLK), jnp.float32)

    def ahead(step, slot):
        first = step * per_step
        lanes = range(per_step)
        kv = [optics_ref[0, first + i] for i in lanes]
        ko = [optics_ref[1, first + i] for i in lanes]
        kr = [optics_ref[2, first + i] for i in lanes]
        t = [LOG2E * jnp.log(jnp.full((ROWS, BLK), flux_ref[first + i], jnp.float32)) for i in lanes]
        half = 0.5 * rows[0]
        ratio = [None] * per_step
        rest = [None] * per_step
        filled = [None] * per_step
        for level in range(levels):
            last = level == levels - 1
            f0, f1, f2, cs, ca = [packed[k, level] for k in range(5)]
            if not last:
                f5, f6 = packed[5, level], packed[6, level]
            for i in lanes:
                s = kr[i] * f0 + cs
                a = kv[i] * f1 + (ko[i] * f2 + ca)
                t[i] = t[i] + (s + a)
                d = jnp.exp2(t[i])
                c = half if last else kr[i] * f5 + f6
                q = a + (half if level == 0 else ratio[i] * rest[i])
                inverse = pl.reciprocal(q + c, approx=True)
                z = ((s + rows[1]) if last else s) * d
                if level > 0:
                    z = z + ratio[i] * filled[i]
                rest[i], filled[i] = q, z
                ratio[i] = c * inverse
                slot[0, level, i] = a
                slot[1, level, i] = d
                slot[2, level, i] = z * inverse
                if not last:
                    slot[3, level, i] = ratio[i]
            yield

    def back(slot):
        x = [None] * per_step
        for level in reversed(range(levels)):
            heat = total[level]
            for i in range(per_step):
                y = slot[2, level, i]
                x[i] = y if level == levels - 1 else y + slot[3, level, i] * x[i]
                heat = heat + slot[0, level, i] * (x[i] + slot[1, level, i])
            total[level] = heat
            yield

    def run(*parts):
        for _ in zip(*parts):
            pass

    steps = bands // per_step
    run(ahead(0, slot_a))

    def two_steps(k, carry):
        run(ahead(2 * k + 1, slot_b), back(slot_a))
        run(ahead(2 * k + 2, slot_a), back(slot_b))
        return carry

    lax.fori_loop(0, (steps - 1) // 2, two_steps, 0)
    if steps % 2:
        run(back(slot_a))
    else:
        run(ahead(steps - 1, slot_b), back(slot_a))
        run(back(slot_b))

    for level in range(levels):
        turned[pl.ds(level, ROWS, stride=levels), :] = total[level]
    half_levels = levels // 2
    for b in range(ROWS):
        cols = pl.ds(b * BLK, BLK)
        cosine = surface_ref[0:1, cols].astype(jnp.float32)
        routed = (routing_ref[group * ROWS + b] >= 0).astype(jnp.float32)
        lit = sunlit_ref[b : b + 1, :].astype(jnp.float32) * routed
        weight = lit * (cosine * cosine) * (-1.0 / (LOG2E * G))
        mine = pl.multiple_of(b * levels + core * half_levels, half_levels)
        other = pl.multiple_of(b * levels + (1 - core) * half_levels, half_levels)
        keep_ref[:, cols] = turned[pl.ds(mine, half_levels), :] * weight
        send_ref[:, cols] = turned[pl.ds(other, half_levels), :] * weight


def solve_groups(core, routing, optics, flux, fields, surface, sunlit, group_of, count, per_step):
    levels = fields.shape[1]
    bands = flux.shape[0]
    half_levels = levels // 2
    smem = pl.BlockSpec(memory_space=pltpu.SMEM)
    out = pl.BlockSpec((half_levels, WIDE), lambda i: (0, i))
    shape = jax.ShapeDtypeStruct((half_levels, count * WIDE), jnp.float32)
    elements = count * WIDE * levels * bands
    return pl.pallas_call(
        functools.partial(solve_kernel, levels, per_step, group_of),
        grid=(count,),
        in_specs=[
            smem,
            smem,
            smem,
            smem,
            pl.BlockSpec((6, levels, WIDE), lambda i: (0, 0, group_of(i))),
            pl.BlockSpec((2, WIDE), lambda i: (0, group_of(i))),
            pl.BlockSpec((ROWS, BLK), lambda i: (group_of(i), 0)),
        ],
        out_specs=[out, out],
        out_shape=[shape, shape],
        scratch_shapes=[
            pltpu.VMEM((5, ROWS * levels, BLK), jnp.float32),
            pltpu.VMEM((7, levels, ROWS, BLK), jnp.float32),
            pltpu.VMEM((2, ROWS, BLK), jnp.float32),
            pltpu.VMEM((levels, ROWS, BLK), jnp.float32),
            pltpu.VMEM((ROWS * levels, BLK), jnp.float32),
            pltpu.VMEM((4, levels, per_step, ROWS, BLK), jnp.float32),
            pltpu.VMEM((4, levels, per_step, ROWS, BLK), jnp.float32),
        ],
        cost_estimate=pl.CostEstimate(
            flops=elements * 24, bytes_accessed=count * WIDE * levels * 20, transcendentals=elements * 2
        ),
    )(core, routing, optics, flux, fields, surface, sunlit)


def exchange_kernel(keep_ref, send_ref, wide_ref, near_ref, halo_ref, own_sem, send_sem, recv_sem):
    count = lax.axis_size("cell")
    cell = lax.axis_index("cell")
    core = lax.axis_index("gpt")
    columns = keep_ref.shape[1]
    after, before = lax.rem(cell + 1, count), lax.rem(cell + count - 1, count)
    partners = [(cell, 1 - core), (after, core), (after, 1 - core), (before, core), (before, 1 - core)]
    middle = pl.ds(HW, columns)
    own = pltpu.make_async_copy(keep_ref, wide_ref.at[:, middle], own_sem)
    own.start()
    barrier = pltpu.get_barrier_semaphore()
    for partner in partners:
        pl.semaphore_signal(barrier, inc=1, device_id=partner, device_id_type=pl.DeviceIdType.MESH)
    pl.semaphore_wait(barrier, len(partners))
    tail = pl.ds(columns - HW, HW)
    head = pl.ds(0, HW)
    copies = [
        (keep_ref.at[:, tail], halo_ref.at[0]),
        (send_ref.at[:, tail], halo_ref.at[1]),
        (keep_ref.at[:, head], halo_ref.at[2]),
        (send_ref.at[:, head], halo_ref.at[3]),
        (send_ref, near_ref),
    ]
    started = []
    for k, (source, target) in enumerate(copies):
        copy = pltpu.make_async_remote_copy(
            src_ref=source,
            dst_ref=target,
            send_sem=send_sem.at[k],
            recv_sem=recv_sem.at[k],
            device_id=(partners[1:] + partners[:1])[k],
            device_id_type=pl.DeviceIdType.MESH,
        )
        copy.start()
        started.append(copy)
    own.wait()
    for copy in started:
        copy.wait()
    wide_ref[:, 0:HW] = halo_ref[0] + halo_ref[1]
    wide_ref[:, HW + columns : 2 * HW + columns] = halo_ref[2] + halo_ref[3]
    wide_ref[:, middle] = wide_ref[:, middle] + near_ref[...]


def exchange(keep, send):
    half_levels, columns = keep.shape
    return pl.pallas_call(
        exchange_kernel,
        in_specs=[pl.BlockSpec(memory_space=pl.ANY)] * 2,
        out_specs=pl.BlockSpec(memory_space=pltpu.VMEM),
        out_shape=jax.ShapeDtypeStruct((half_levels, columns + 2 * HW), jnp.float32),
        scratch_shapes=[
            pltpu.VMEM((half_levels, columns), jnp.float32),
            pltpu.VMEM((4, half_levels, HW), jnp.float32),
            pltpu.SemaphoreType.DMA,
            pltpu.SemaphoreType.DMA((5,)),
            pltpu.SemaphoreType.DMA((5,)),
        ],
        compiler_params=pltpu.CompilerParams(collective_id=0, has_side_effects=True),
    )(keep, send)


def interpolate_kernel(wide, stencil_ref, weights_ref, out_ref):
    columns = out_ref.shape[1]
    points = stencil_ref.shape[0]
    blocks = columns // BLK
    base = pl.program_id(0) * columns
    lane = lax.broadcasted_iota(jnp.int32, (points, BLK), 1) + HW

    def one_block(block, carry):
        start = pl.multiple_of(block * BLK, BLK)
        weights = weights_ref[:, pl.ds(start, BLK)]
        shares = weights / jnp.sum(weights, axis=0, keepdims=True)
        place = stencil_ref[:, pl.ds(start, BLK)] + lane
        which = place >> 7
        inner = place & (BLK - 1)
        sources = [wide[:, pl.ds(pl.multiple_of(base + start + k * BLK, BLK), BLK)] for k in range(3)]
        result = jnp.zeros(sources[0].shape, jnp.float32)
        for j in range(points):
            index = jnp.broadcast_to(inner[j : j + 1, :], result.shape)
            part = jnp.broadcast_to(which[j : j + 1, :], result.shape)
            got = [jnp.take_along_axis(s, index, axis=1, mode="promise_in_bounds") for s in sources]
            value = jnp.where(part == 0, got[0], jnp.where(part == 1, got[1], got[2]))
            result = result + shares[j : j + 1, :] * value
        out_ref[:, pl.ds(start, BLK)] = result
        return carry

    lax.fori_loop(0, blocks, one_block, 0, unroll=8)


def interpolate(wide, stencil, weights):
    half_levels = wide.shape[0]
    points, columns = stencil.shape
    part = 4 * WIDE
    piece = pl.BlockSpec((points, part), lambda i: (0, i))
    return pl.pallas_call(
        interpolate_kernel,
        grid=(columns // part,),
        in_specs=[pl.BlockSpec(memory_space=pltpu.VMEM), piece, piece],
        out_specs=pl.BlockSpec((half_levels, part), lambda i: (0, i)),
        out_shape=jax.ShapeDtypeStruct((half_levels, columns), jnp.float32),
    )(wide, stencil, weights)


def local(fields, surface, sunlit, routing, stencil, weights, optics, solar_flux):
    columns = fields.shape[2]
    groups = columns // WIDE
    core = lax.axis_index("gpt").reshape(1)
    lit = sunlit.reshape(columns // BLK, BLK)
    solve = functools.partial(solve_groups, core, routing, optics, solar_flux, fields, surface, lit)
    keep, send = solve(lambda i: i, groups, 4)
    return interpolate(exchange(keep, send), stencil, weights)


def solution(mesh):
    placed = (
        P(None, None, "cell"),
        P(None, "cell"),
        P("cell"),
        P("cell"),
        P(None, "cell"),
        P(None, "cell"),
        P(None, "gpt"),
        P("gpt"),
    )
    return jax.shard_map(
        local, mesh=mesh, in_specs=placed, out_specs=P("gpt", "cell"), check_vma=False
    )
```
